32 devices in a mesh: row: 4 (over z), col: 8 (over y, x, core).
Axes of the slice: x: 2, y: 2, z: 4, core: 2. Of those that a mesh axis runs over, the one named last changes fastest.
Arguments:
- sources: float32 [30, 4096], P(None, ('row', 'col')), may hold values from -12 to 12
- log_source_mass: float32 [4096], P(('row', 'col')), may hold values from -4 to 4
- targets: float32 [30, 4096], P(None, 'col'), may hold values from -6 to 6
- log_target_mass: float32 [4096], P('col'), may hold values from -4 to 4
- start_potential: float32 [4096], P('col'), may hold values from -12 to 250
Outputs:
- row_potential: float32 [4096], P(('row', 'col'))
- column_potential: float32 [4096], P('col')
The draws below stay inside these ranges and needn't reach their ends.
All inputs are finite; a program needn't handle non-finite values.
Results may differ from the reference program's by a relative error of at most 0.00015.
Values sent between devices are 32-bit elements; how exact they have to be, the bound alone decides.
A program may use at most 64 MiB of HBM per device.

```python
import jax
import jax.numpy as jnp
from jax import lax

D = 30
ITERS = 2
SRC = 4096
TGT = 4096


def draw_sources(key, part):
    base = jax.random.normal(jax.random.fold_in(key, 11), (D, SRC), jnp.float32)
    return jnp.clip(base, -12.0, 12.0)


def draw_start_potential(key, part):
    base = 2.0 * jax.random.normal(jax.random.fold_in(key, 21), (TGT,), jnp.float32)
    return jnp.clip(base, -12.0, 250.0)


def levels(stream_key, extent, pieces, least, largest):
    factor_of, own = 1.0, jax.random.fold_in(stream_key, 6)
    for axis_at, parts in pieces:
        steps = jnp.exp(jax.random.uniform(jax.random.fold_in(own, axis_at), (parts,), jnp.float32, least / len(pieces), largest / len(pieces)))
        factor_of = factor_of * jnp.repeat(steps, extent[axis_at] // parts).reshape([-1 if axis == axis_at else 1 for axis in range(len(extent))])
    return factor_of


def scatter_about(stream_key, extent, width, most, cuts=(), dtype=jnp.bfloat16):
    result = jax.random.normal(stream_key, extent, jnp.float32) * width
    if len(cuts) > 0:
        result = levels(stream_key, extent, cuts, -0.22, 0.18) * result
    return jnp.clip(result, min=-most, max=most).astype(dtype)


def setup_inputs(seed: int = 0) -> dict:
    splits = jax.random.split(jax.random.key(seed), 6)
    return {
        "sources": draw_sources(jax.random.fold_in(splits[5], 71), 0),
        "log_source_mass": scatter_about(splits[1], (SRC,), 1.0, 4.0, ((0, 32),), jnp.float32),
        "targets": scatter_about(splits[2], (D, TGT), 1.0, 6.0, ((1, 8),), jnp.float32),
        "log_target_mass": scatter_about(splits[3], (TGT,), 1.0, 4.0, ((0, 8),), jnp.float32),
        "start_potential": draw_start_potential(jax.random.fold_in(splits[5], 71), 0),
    }


entropic_scale = 2.0


def row_sweep(sources, targets, target_term):
    dims, count = sources.shape
    block_rows = 256 if count % 256 == 0 else count
    target_sq = 0.5 * jnp.sum(targets * targets, axis=0)
    blocks = sources.T.reshape(count // block_rows, block_rows, dims)

    def one_block(coords):
        inner = jnp.dot(coords, targets, precision=lax.Precision.HIGHEST, preferred_element_type=jnp.float32)
        cost = 0.5 * jnp.sum(coords * coords, axis=1)[:, None] + target_sq[None, :] - inner
        return jax.nn.logsumexp(target_term[None, :] - cost / entropic_scale, axis=1)

    return (-entropic_scale * lax.map(one_block, blocks)).reshape(count)


def reference(sources, log_source_mass, targets, log_target_mass, start_potential):
    target_term = start_potential / entropic_scale + log_target_mass
    row_potential = jnp.zeros((sources.shape[1],), jnp.float32)
    column_potential = start_potential
    for sweep in range(ITERS):
        row_potential = row_sweep(sources, targets, target_term)
        source_term = row_potential / entropic_scale + log_source_mass
        column_potential = row_sweep(targets, sources, source_term)
        target_term = column_potential / entropic_scale + log_target_mass
    return row_potential, column_potential
```

```python
import functools

import jax
import jax.numpy as jnp
from jax import lax
from jax.experimental import pallas as pl
from jax.experimental.pallas import tpu as pltpu
from jax.sharding import PartitionSpec as P

ITERS = 2
MESH = pl.DeviceIdType.MESH
LANES = 128
EXTRA = 16
LOG2E = 1.4426950408889634
LN2 = 0.6931471805599453


def split3(x):
    hi = x.astype(jnp.bfloat16).astype(jnp.float32)
    rest = x - hi
    mid = rest.astype(jnp.bfloat16).astype(jnp.float32)
    return hi, mid, rest - mid


def term_rows(term):
    hi, mid, low = split3(term)
    row = lax.broadcasted_iota(jnp.int32, (EXTRA, term.shape[1]), 0)
    zero = jnp.zeros((EXTRA, term.shape[1]), jnp.float32)
    return jnp.where(row == 0, hi, jnp.where(row == 1, mid, jnp.where(row == 2, low, zero))).astype(jnp.bfloat16)


def one_rows(n):
    row = lax.broadcasted_iota(jnp.int32, (EXTRA, n), 0)
    return jnp.where(row < 3, 1.0, 0.0).astype(jnp.bfloat16)


def merge(parts):
    peak = parts[0]
    for part in parts[1:]:
        peak = jnp.maximum(peak, part)
    total = jnp.exp2(parts[0] - peak)
    for part in parts[1:]:
        total = total + jnp.exp2(part - peak)
    return peak + jnp.log2(total)


def column_lse(left, right, lo, hi, out, slot):
    width = right.shape[1]
    step = 256 if width % 256 == 0 else LANES
    for at in range(0, width, step):
        scores = lax.dot_general(
            left[lo:hi, :],
            right[lo:hi, at : at + step],
            (((0,), (0,)), ((), ())),
            preferred_element_type=jnp.float32,
        )
        peak = jnp.max(scores, axis=0, keepdims=True)
        total = jnp.sum(jnp.exp2(scores - peak), axis=0, keepdims=True)
        part = peak + jnp.log2(total)
        for k in range(step // LANES):
            b = at // LANES + k
            out[slot, b : b + 1, :] = part[:, k * LANES : (k + 1) * LANES]


def kernel(
    nr, nc, src, lsm, tgt, ltm, pot, row_out, col_out,
    gathered, left, right, lsm2, row_lse, row_parts, col_parts,
    gather_send, gather_recv, row_send, row_recv, col_send, col_recv,
):
    r, c = lax.axis_index("row"), lax.axis_index("col")
    dims, own = src.shape
    height = gathered.shape[1]
    cols = tgt.shape[1]
    row_blocks, col_blocks = nc * own // LANES, cols // LANES
    per = own // LANES

    barrier = pltpu.get_barrier_semaphore()
    for d in range(1, nc):
        pl.semaphore_signal(barrier, inc=1, device_id=(r, lax.rem(c + d, nc)), device_id_type=MESH)
    for d in range(1, nr):
        pl.semaphore_signal(barrier, inc=1, device_id=(lax.rem(r + d, nr), c), device_id_type=MESH)

    gathered[c, 0:dims, :] = src[...]
    for q in range(per):
        gathered[c, dims : dims + 1, q * LANES : (q + 1) * LANES] = lsm[q : q + 1, :]
    gathered[c, dims + 1 : height, :] = jnp.zeros((height - dims - 1, own), jnp.float32)

    pl.semaphore_wait(barrier, nc + nr - 2)

    def along_col(buf, send, recv, d):
        return pltpu.make_async_remote_copy(
            src_ref=buf.at[c], dst_ref=buf.at[c], send_sem=send.at[d - 1], recv_sem=recv.at[d - 1],
            device_id=(r, lax.rem(c + d, nc)), device_id_type=MESH,
        )

    def along_row(buf, send, recv, d):
        return pltpu.make_async_remote_copy(
            src_ref=buf.at[r], dst_ref=buf.at[r], send_sem=send.at[d - 1], recv_sem=recv.at[d - 1],
            device_id=(lax.rem(r + d, nr), c), device_id_type=MESH,
        )

    copies = [along_col(gathered, gather_send, gather_recv, d) for d in range(1, nc)]
    for copy in copies:
        copy.start()

    lead = EXTRA
    tail = EXTRA + 6 * height
    coords = jnp.concatenate([tgt[...], jnp.zeros((height - dims, cols), jnp.float32)], axis=0)
    t1, t2, t3 = [part.astype(jnp.bfloat16) for part in split3(coords)]
    for k, part in enumerate((t1, t1, t2, t2, t1, t3)):
        left[lead + k * height : lead + (k + 1) * height, :] = part
    left[tail : tail + EXTRA, :] = one_rows(cols)
    target_sq = jnp.sum(coords * coords, axis=0, keepdims=True)
    for b in range(col_blocks):
        at = slice(b * LANES, (b + 1) * LANES)
        term = (0.5 * pot[b : b + 1, :] + ltm[b : b + 1, :]) * LOG2E - (0.25 * LOG2E) * target_sq[:, at]
        left[0:EXTRA, at] = term_rows(term)
    right[0:EXTRA, :] = one_rows(nc * own)

    for copy in copies:
        copy.wait()

    for k in range(nc):
        at = slice(k * own, (k + 1) * own)
        block = gathered[k]
        for q in range(per):
            b = k * per + q
            lsm2[b : b + 1, :] = block[dims : dims + 1, q * LANES : (q + 1) * LANES] * LOG2E
        s1, s2, s3 = [part.astype(jnp.bfloat16) for part in split3(block * (0.5 * LOG2E))]
        for g, part in enumerate((s1, s2, s1, s2, s3, s1)):
            right[lead + g * height : lead + (g + 1) * height, at] = part

    for sweep in range(ITERS):
        parts = row_parts.at[sweep]
        column_lse(left, right, 0, tail, parts, c)
        copies = [along_col(parts, row_send.at[sweep], row_recv.at[sweep], d) for d in range(1, nc)]
        for copy in copies:
            copy.start()
        for copy in copies:
            copy.wait()
        lse = merge([parts[k] for k in range(nc)])
        if sweep == ITERS - 1:
            row_lse[...] = lse
        term = lsm2[...] - lse
        for b in range(row_blocks):
            right[tail : tail + EXTRA, b * LANES : (b + 1) * LANES] = term_rows(term[b : b + 1, :])

        parts = col_parts.at[sweep]
        column_lse(right, left, lead, tail + EXTRA, parts, r)
        copies = [along_row(parts, col_send.at[sweep], col_recv.at[sweep], d) for d in range(1, nr)]
        for copy in copies:
            copy.start()
        if sweep == ITERS - 1:
            own_sq = jnp.sum(src[...] * src[...], axis=0, keepdims=True)
            for q in range(per):
                row_out[q : q + 1, :] = (
                    0.5 * own_sq[:, q * LANES : (q + 1) * LANES]
                    - (2.0 * LN2) * row_lse[pl.ds(c * per + q, 1), :]
                )
        for copy in copies:
            copy.wait()
        lse = merge([parts[k] for k in range(nr)])
        if sweep < ITERS - 1:
            term = ltm[...] * LOG2E - lse
            for b in range(col_blocks):
                left[0:EXTRA, b * LANES : (b + 1) * LANES] = term_rows(term[b : b + 1, :])
        else:
            for b in range(col_blocks):
                at = slice(b * LANES, (b + 1) * LANES)
                col_out[b : b + 1, :] = 0.5 * target_sq[:, at] - (2.0 * LN2) * lse[b : b + 1, :]


def on_device(nr, nc, sources, log_source_mass, targets, log_target_mass, start_potential):
    dims, own = sources.shape
    cols = targets.shape[1]
    height = -(-(dims + 2) // EXTRA) * EXTRA
    deep = 6 * height + 2 * EXTRA
    row_blocks, col_blocks = nc * own // LANES, cols // LANES
    vmem = pl.BlockSpec(memory_space=pltpu.VMEM)
    row, col = pl.pallas_call(
        functools.partial(kernel, nr, nc),
        out_shape=(
            jax.ShapeDtypeStruct((own // LANES, LANES), jnp.float32),
            jax.ShapeDtypeStruct((col_blocks, LANES), jnp.float32),
        ),
        in_specs=[vmem] * 5,
        out_specs=(vmem, vmem),
        scratch_shapes=[
            pltpu.VMEM((nc, height, own), jnp.float32),
            pltpu.VMEM((deep, cols), jnp.bfloat16),
            pltpu.VMEM((deep, nc * own), jnp.bfloat16),
            pltpu.VMEM((row_blocks, LANES), jnp.float32),
            pltpu.VMEM((row_blocks, LANES), jnp.float32),
            pltpu.VMEM((ITERS, nc, row_blocks, LANES), jnp.float32),
            pltpu.VMEM((ITERS, nr, col_blocks, LANES), jnp.float32),
            pltpu.SemaphoreType.DMA((nc - 1,)),
            pltpu.SemaphoreType.DMA((nc - 1,)),
            pltpu.SemaphoreType.DMA((ITERS, nc - 1)),
            pltpu.SemaphoreType.DMA((ITERS, nc - 1)),
            pltpu.SemaphoreType.DMA((ITERS, nr - 1)),
            pltpu.SemaphoreType.DMA((ITERS, nr - 1)),
        ],
        compiler_params=pltpu.CompilerParams(
            collective_id=0, has_side_effects=True, vmem_limit_bytes=48 * 1024 * 1024
        ),
    )(
        sources,
        log_source_mass.reshape(own // LANES, LANES),
        targets,
        log_target_mass.reshape(col_blocks, LANES),
        start_potential.reshape(col_blocks, LANES),
    )
    return row.reshape(own), col.reshape(cols)


def solution(mesh):
    return jax.shard_map(
        functools.partial(on_device, mesh.shape["row"], mesh.shape["col"]),
        mesh=mesh,
        in_specs=(P(None, ("row", "col")), P(("row", "col")), P(None, "col"), P("col"), P("col")),
        out_specs=(P(("row", "col")), P("col")),
        check_vma=False,
    )
```

```python
import functools

import jax
import jax.numpy as jnp
from jax import lax
from jax.experimental import pallas as pl
from jax.experimental.pallas import tpu as pltpu
from jax.sharding import PartitionSpec as P

ITERS = 2
MESH = pl.DeviceIdType.MESH
LANES = 128
EXTRA = 16
LOG2E = 1.4426950408889634
LN2 = 0.6931471805599453


def split3(x):
    hi = x.astype(jnp.bfloat16).astype(jnp.float32)
    rest = x - hi
    mid = rest.astype(jnp.bfloat16).astype(jnp.float32)
    return hi, mid, rest - mid


def term_rows(term):
    hi, mid, low = split3(term)
    row = lax.broadcasted_iota(jnp.int32, (EXTRA, term.shape[1]), 0)
    zero = jnp.zeros((EXTRA, term.shape[1]), jnp.float32)
    return jnp.where(row == 0, hi, jnp.where(row == 1, mid, jnp.where(row == 2, low, zero))).astype(jnp.bfloat16)


def one_rows(n):
    row = lax.broadcasted_iota(jnp.int32, (EXTRA, n), 0)
    return jnp.where(row < 3, 1.0, 0.0).astype(jnp.bfloat16)


def merge(parts):
    peak = parts[0]
    for part in parts[1:]:
        peak = jnp.maximum(peak, part)
    total = jnp.exp2(parts[0] - peak)
    for part in parts[1:]:
        total = total + jnp.exp2(part - peak)
    return peak + jnp.log2(total)


def column_lse(left, right, lo, hi, out, slot):
    width = right.shape[1]
    step = 256 if width % 256 == 0 else LANES
    for at in range(0, width, step):
        scores = lax.dot_general(
            left[lo:hi, :],
            right[lo:hi, at : at + step],
            (((0,), (0,)), ((), ())),
            preferred_element_type=jnp.float32,
        )
        peak = jnp.max(scores, axis=0, keepdims=True)
        total = jnp.sum(jnp.exp2(scores - peak), axis=0, keepdims=True)
        part = peak + jnp.log2(total)
        for k in range(step // LANES):
            b = at // LANES + k
            out[slot, b : b + 1, :] = part[:, k * LANES : (k + 1) * LANES]


def kernel(
    nr, nc, src_in, lsm_in, tgt_in, ltm_in, pot_in, row_out, col_out,
    src, lsm, tgt, ltm, pot, load_sem, gathered, left, right, lsm2, row_lse, row_parts, col_parts,
    gather_send, gather_recv, row_send, row_recv, col_send, col_recv,
):
    r, c = lax.axis_index("row"), lax.axis_index("col")
    barrier = pltpu.get_barrier_semaphore()
    for d in range(1, nc):
        pl.semaphore_signal(barrier, inc=1, device_id=(r, lax.rem(c + d, nc)), device_id_type=MESH)
    for d in range(1, nr):
        pl.semaphore_signal(barrier, inc=1, device_id=(lax.rem(r + d, nr), c), device_id_type=MESH)

    loads = [
        pltpu.make_async_copy(here, there, load_sem.at[k])
        for k, (here, there) in enumerate(
            ((src_in, src), (lsm_in, lsm), (tgt_in, tgt), (ltm_in, ltm), (pot_in, pot))
        )
    ]
    for load in loads:
        load.start()
    dims, own = src.shape
    height = gathered.shape[1]
    cols = tgt.shape[1]
    row_blocks, col_blocks = nc * own // LANES, cols // LANES
    per = own // LANES

    loads[0].wait()
    loads[1].wait()
    gathered[c, 0:dims, :] = src[...]
    for q in range(per):
        gathered[c, dims : dims + 1, q * LANES : (q + 1) * LANES] = lsm[q : q + 1, :]
    gathered[c, dims + 1 : height, :] = jnp.zeros((height - dims - 1, own), jnp.float32)

    pl.semaphore_wait(barrier, nc + nr - 2)

    def along_col(buf, send, recv, d):
        return pltpu.make_async_remote_copy(
            src_ref=buf.at[c], dst_ref=buf.at[c], send_sem=send.at[d - 1], recv_sem=recv.at[d - 1],
            device_id=(r, lax.rem(c + d, nc)), device_id_type=MESH,
        )

    def along_row(buf, send, recv, d):
        return pltpu.make_async_remote_copy(
            src_ref=buf.at[r], dst_ref=buf.at[r], send_sem=send.at[d - 1], recv_sem=recv.at[d - 1],
            device_id=(lax.rem(r + d, nr), c), device_id_type=MESH,
        )

    copies = [along_col(gathered, gather_send, gather_recv, d) for d in range(1, nc)]
    for copy in copies:
        copy.start()

    for load in loads[2:]:
        load.wait()

    lead = EXTRA
    tail = EXTRA + 6 * height
    coords = jnp.concatenate([tgt[...], jnp.zeros((height - dims, cols), jnp.float32)], axis=0)
    t1, t2, t3 = [part.astype(jnp.bfloat16) for part in split3(coords)]
    for k, part in enumerate((t1, t1, t2, t2, t1, t3)):
        left[lead + k * height : lead + (k + 1) * height, :] = part
    left[tail : tail + EXTRA, :] = one_rows(cols)
    target_sq = jnp.sum(coords * coords, axis=0, keepdims=True)
    for b in range(col_blocks):
        at = slice(b * LANES, (b + 1) * LANES)
        term = (0.5 * pot[b : b + 1, :] + ltm[b : b + 1, :]) * LOG2E - (0.25 * LOG2E) * target_sq[:, at]
        left[0:EXTRA, at] = term_rows(term)
    right[0:EXTRA, :] = one_rows(nc * own)

    for copy in copies:
        copy.wait_recv()

    for k in range(nc):
        at = slice(k * own, (k + 1) * own)
        block = gathered[k]
        for q in range(per):
            b = k * per + q
            lsm2[b : b + 1, :] = block[dims : dims + 1, q * LANES : (q + 1) * LANES] * LOG2E
        s1, s2, s3 = [part.astype(jnp.bfloat16) for part in split3(block * (0.5 * LOG2E))]
        for g, part in enumerate((s1, s2, s1, s2, s3, s1)):
            right[lead + g * height : lead + (g + 1) * height, at] = part

    sent = copies
    for sweep in range(ITERS):
        parts = row_parts.at[sweep]
        column_lse(left, right, 0, tail, parts, c)
        copies = [along_col(parts, row_send.at[sweep], row_recv.at[sweep], d) for d in range(1, nc)]
        for copy in copies:
            copy.start()
        for copy in copies:
            copy.wait_recv()
        sent += copies
        lse = merge([parts[k] for k in range(nc)])
        if sweep == ITERS - 1:
            row_lse[...] = lse
        term = lsm2[...] - lse
        for b in range(row_blocks):
            right[tail : tail + EXTRA, b * LANES : (b + 1) * LANES] = term_rows(term[b : b + 1, :])

        parts = col_parts.at[sweep]
        column_lse(right, left, lead, tail + EXTRA, parts, r)
        copies = [along_row(parts, col_send.at[sweep], col_recv.at[sweep], d) for d in range(1, nr)]
        for copy in copies:
            copy.start()
        if sweep == ITERS - 1:
            own_sq = jnp.sum(src[...] * src[...], axis=0, keepdims=True)
            for q in range(per):
                row_out[q : q + 1, :] = (
                    0.5 * own_sq[:, q * LANES : (q + 1) * LANES]
                    - (2.0 * LN2) * row_lse[pl.ds(c * per + q, 1), :]
                )
        for copy in copies:
            copy.wait_recv()
        sent += copies
        lse = merge([parts[k] for k in range(nr)])
        if sweep < ITERS - 1:
            term = ltm[...] * LOG2E - lse
            for b in range(col_blocks):
                left[0:EXTRA, b * LANES : (b + 1) * LANES] = term_rows(term[b : b + 1, :])
        else:
            for b in range(col_blocks):
                at = slice(b * LANES, (b + 1) * LANES)
                col_out[b : b + 1, :] = 0.5 * target_sq[:, at] - (2.0 * LN2) * lse[b : b + 1, :]
    for copy in sent:
        copy.wait_send()


def on_device(nr, nc, sources, log_source_mass, targets, log_target_mass, start_potential):
    dims, own = sources.shape
    cols = targets.shape[1]
    height = -(-(dims + 2) // EXTRA) * EXTRA
    deep = 6 * height + 2 * EXTRA
    row_blocks, col_blocks = nc * own // LANES, cols // LANES
    vmem = pl.BlockSpec(memory_space=pltpu.VMEM)
    row, col = pl.pallas_call(
        functools.partial(kernel, nr, nc),
        out_shape=(
            jax.ShapeDtypeStruct((own // LANES, LANES), jnp.float32),
            jax.ShapeDtypeStruct((col_blocks, LANES), jnp.float32),
        ),
        in_specs=[pl.BlockSpec(memory_space=pltpu.HBM)] * 5,
        out_specs=(vmem, vmem),
        scratch_shapes=[
            pltpu.VMEM((dims, own), jnp.float32),
            pltpu.VMEM((own // LANES, LANES), jnp.float32),
            pltpu.VMEM((dims, cols), jnp.float32),
            pltpu.VMEM((col_blocks, LANES), jnp.float32),
            pltpu.VMEM((col_blocks, LANES), jnp.float32),
            pltpu.SemaphoreType.DMA((5,)),
            pltpu.VMEM((nc, height, own), jnp.float32),
            pltpu.VMEM((deep, cols), jnp.bfloat16),
            pltpu.VMEM((deep, nc * own), jnp.bfloat16),
            pltpu.VMEM((row_blocks, LANES), jnp.float32),
            pltpu.VMEM((row_blocks, LANES), jnp.float32),
            pltpu.VMEM((ITERS, nc, row_blocks, LANES), jnp.float32),
            pltpu.VMEM((ITERS, nr, col_blocks, LANES), jnp.float32),
            pltpu.SemaphoreType.DMA((nc - 1,)),
            pltpu.SemaphoreType.DMA((nc - 1,)),
            pltpu.SemaphoreType.DMA((ITERS, nc - 1)),
            pltpu.SemaphoreType.DMA((ITERS, nc - 1)),
            pltpu.SemaphoreType.DMA((ITERS, nr - 1)),
            pltpu.SemaphoreType.DMA((ITERS, nr - 1)),
        ],
        compiler_params=pltpu.CompilerParams(
            collective_id=0, has_side_effects=True, vmem_limit_bytes=48 * 1024 * 1024
        ),
    )(
        hbm(sources),
        hbm(log_source_mass.reshape(own // LANES, LANES)),
        hbm(targets),
        hbm(log_target_mass.reshape(col_blocks, LANES)),
        hbm(start_potential.reshape(col_blocks, LANES)),
    )
    return row.reshape(own), col.reshape(cols)


def hbm(x):
    return pltpu.with_memory_space_constraint(x, pltpu.HBM)


def solution(mesh):
    return jax.shard_map(
        functools.partial(on_device, mesh.shape["row"], mesh.shape["col"]),
        mesh=mesh,
        in_specs=(P(None, ("row", "col")), P(("row", "col")), P(None, "col"), P("col"), P("col")),
        out_specs=(P(("row", "col")), P("col")),
        check_vma=False,
    )
```

```python
import functools

import jax
import jax.numpy as jnp
from jax import lax
from jax.experimental import pallas as pl
from jax.experimental.pallas import tpu as pltpu
from jax.sharding import PartitionSpec as P

ITERS = 2
MESH = pl.DeviceIdType.MESH
LANES = 128
EXTRA = 16
LOG2E = 1.4426950408889634
LN2 = 0.6931471805599453
LEFT = (0, 0, 1, 1, 0, 2)
RIGHT = (0, 1, 0, 1, 2, 0)


def split3(x):
    hi = x.astype(jnp.bfloat16).astype(jnp.float32)
    rest = x - hi
    mid = rest.astype(jnp.bfloat16).astype(jnp.float32)
    return hi, mid, rest - mid


def term_rows(term):
    hi, mid, low = split3(term)
    row = lax.broadcasted_iota(jnp.int32, (EXTRA, term.shape[1]), 0)
    zero = jnp.zeros((EXTRA, term.shape[1]), jnp.float32)
    return jnp.where(row == 0, hi, jnp.where(row == 1, mid, jnp.where(row == 2, low, zero)))


def one_rows(n):
    row = lax.broadcasted_iota(jnp.int32, (EXTRA, n), 0)
    return jnp.where(row < 3, 1.0, 0.0).astype(jnp.bfloat16)


def merge(parts):
    peak = parts[0]
    for part in parts[1:]:
        peak = jnp.maximum(peak, part)
    total = jnp.exp2(parts[0] - peak)
    for part in parts[1:]:
        total = total + jnp.exp2(part - peak)
    return peak + jnp.log2(total)


def column_lse(left_t, right, out, slot):
    width = right.shape[1]
    step = 256 if width % 256 == 0 else LANES
    for at in range(0, width, step):
        scores = jnp.dot(left_t[...], right[:, at : at + step], preferred_element_type=jnp.float32)
        peak = jnp.max(scores, axis=0, keepdims=True)
        total = jnp.sum(jnp.exp2(scores - peak), axis=0, keepdims=True)
        part = peak + jnp.log2(total)
        for k in range(step // LANES):
            b = at // LANES + k
            out[slot, b : b + 1, :] = part[:, k * LANES : (k + 1) * LANES]


def turn_coords(parts, order, out):
    for b in range(out.shape[0] // LANES):
        blocks = [part[:, b * LANES : (b + 1) * LANES] for part in parts]
        at = slice(b * LANES, (b + 1) * LANES)
        width = 0
        per = LANES // blocks[0].shape[0]
        for first in range(0, len(order), per):
            stack = jnp.concatenate([blocks[k] for k in order[first : first + per]], axis=0)
            out[at, width : width + stack.shape[0]] = stack.T.astype(jnp.bfloat16)
            width += stack.shape[0]


def turn_term(term, out, tail):
    for b in range(term.shape[0]):
        out[b * LANES : (b + 1) * LANES, tail : tail + EXTRA] = term_rows(term[b : b + 1, :]).T.astype(jnp.bfloat16)


def kernel(
    nr, nc, src_in, lsm_in, tgt_in, ltm_in, pot_in, row_out, col_out,
    src, lsm, tgt, ltm, pot, load_sem, gathered, left, right, left_t, right_t, lsm2, row_lse, row_parts, col_parts,
    gather_send, gather_recv, row_send, row_recv, col_send, col_recv,
):
    r, c = lax.axis_index("row"), lax.axis_index("col")
    barrier = pltpu.get_barrier_semaphore()
    for d in range(1, nc):
        pl.semaphore_signal(barrier, inc=1, device_id=(r, lax.rem(c + d, nc)), device_id_type=MESH)
    for d in range(1, nr):
        pl.semaphore_signal(barrier, inc=1, device_id=(lax.rem(r + d, nr), c), device_id_type=MESH)

    loads = [
        pltpu.make_async_copy(here, there, load_sem.at[k])
        for k, (here, there) in enumerate(
            ((src_in, src), (lsm_in, lsm), (tgt_in, tgt), (ltm_in, ltm), (pot_in, pot))
        )
    ]
    for load in loads:
        load.start()
    dims, own = src.shape
    height = gathered.shape[1]
    cols = tgt.shape[1]
    row_blocks, col_blocks = nc * own // LANES, cols // LANES
    per = own // LANES

    loads[0].wait()
    loads[1].wait()
    gathered[c, 0:dims, :] = src[...]
    for q in range(per):
        gathered[c, dims : dims + 1, q * LANES : (q + 1) * LANES] = lsm[q : q + 1, :]
    gathered[c, dims + 1 : height, :] = jnp.zeros((height - dims - 1, own), jnp.float32)

    pl.semaphore_wait(barrier, nc + nr - 2)

    def along_col(buf, send, recv, d):
        return pltpu.make_async_remote_copy(
            src_ref=buf.at[c], dst_ref=buf.at[c], send_sem=send.at[d - 1], recv_sem=recv.at[d - 1],
            device_id=(r, lax.rem(c + d, nc)), device_id_type=MESH,
        )

    def along_row(buf, send, recv, d):
        return pltpu.make_async_remote_copy(
            src_ref=buf.at[r], dst_ref=buf.at[r], send_sem=send.at[d - 1], recv_sem=recv.at[d - 1],
            device_id=(lax.rem(r + d, nr), c), device_id_type=MESH,
        )

    copies = [along_col(gathered, gather_send, gather_recv, d) for d in range(1, nc)]
    for copy in copies:
        copy.start()

    for load in loads[2:]:
        load.wait()

    tail = 6 * height
    coords = jnp.concatenate([tgt[...], jnp.zeros((height - dims, cols), jnp.float32)], axis=0)
    pieces = split3(coords)
    for k, p in enumerate(LEFT):
        left[k * height : (k + 1) * height, :] = pieces[p].astype(jnp.bfloat16)
    left[tail : tail + EXTRA, :] = one_rows(cols)
    turn_coords(pieces, LEFT, left_t)
    target_sq = jnp.sum(coords * coords, axis=0, keepdims=True)
    target_sq = jnp.concatenate(
        [target_sq[:, b * LANES : (b + 1) * LANES] for b in range(col_blocks)], axis=0
    )
    turn_term((0.5 * pot[...] + ltm[...]) * LOG2E - (0.25 * LOG2E) * target_sq, left_t, tail)
    right[tail : tail + EXTRA, :] = one_rows(nc * own)

    for copy in copies:
        copy.wait_recv()

    for k in range(nc):
        at = slice(k * own, (k + 1) * own)
        block = gathered[k]
        for q in range(per):
            b = k * per + q
            lsm2[b : b + 1, :] = block[dims : dims + 1, q * LANES : (q + 1) * LANES] * LOG2E
        pieces = split3(block * (0.5 * LOG2E))
        for g, p in enumerate(RIGHT):
            right[g * height : (g + 1) * height, at] = pieces[p].astype(jnp.bfloat16)

    sent = copies
    for sweep in range(ITERS):
        parts = row_parts.at[sweep]
        column_lse(left_t, right, parts, c)
        copies = [along_col(parts, row_send.at[sweep], row_recv.at[sweep], d) for d in range(1, nc)]
        for copy in copies:
            copy.start()
        if sweep == 0:
            for k in range(nc):
                turn_coords(split3(gathered[k] * (0.5 * LOG2E)), RIGHT, right_t.at[k * own : (k + 1) * own])
        for copy in copies:
            copy.wait_recv()
        sent += copies
        lse = merge([parts[k] for k in range(nc)])
        if sweep == ITERS - 1:
            row_lse[...] = lse
        turn_term(lsm2[...] - lse, right_t, tail)

        parts = col_parts.at[sweep]
        column_lse(right_t, left, parts, r)
        copies = [along_row(parts, col_send.at[sweep], col_recv.at[sweep], d) for d in range(1, nr)]
        for copy in copies:
            copy.start()
        if sweep == ITERS - 1:
            own_sq = jnp.sum(src[...] * src[...], axis=0, keepdims=True)
            for q in range(per):
                row_out[q : q + 1, :] = (
                    0.5 * own_sq[:, q * LANES : (q + 1) * LANES]
                    - (2.0 * LN2) * row_lse[pl.ds(c * per + q, 1), :]
                )
        for copy in copies:
            copy.wait_recv()
        sent += copies
        lse = merge([parts[k] for k in range(nr)])
        if sweep < ITERS - 1:
            turn_term(ltm[...] * LOG2E - lse, left_t, tail)
        else:
            col_out[...] = 0.5 * target_sq - (2.0 * LN2) * lse
    for copy in sent:
        copy.wait_send()


def on_device(nr, nc, sources, log_source_mass, targets, log_target_mass, start_potential):
    dims, own = sources.shape
    cols = targets.shape[1]
    height = -(-(dims + 2) // EXTRA) * EXTRA
    deep = 6 * height + EXTRA
    row_blocks, col_blocks = nc * own // LANES, cols // LANES
    vmem = pl.BlockSpec(memory_space=pltpu.VMEM)
    row, col = pl.pallas_call(
        functools.partial(kernel, nr, nc),
        out_shape=(
            jax.ShapeDtypeStruct((own // LANES, LANES), jnp.float32),
            jax.ShapeDtypeStruct((col_blocks, LANES), jnp.float32),
        ),
        in_specs=[pl.BlockSpec(memory_space=pltpu.HBM)] * 5,
        out_specs=(vmem, vmem),
        scratch_shapes=[
            pltpu.VMEM((dims, own), jnp.float32),
            pltpu.VMEM((own // LANES, LANES), jnp.float32),
            pltpu.VMEM((dims, cols), jnp.float32),
            pltpu.VMEM((col_blocks, LANES), jnp.float32),
            pltpu.VMEM((col_blocks, LANES), jnp.float32),
            pltpu.SemaphoreType.DMA((5,)),
            pltpu.VMEM((nc, height, own), jnp.float32),
            pltpu.VMEM((deep, cols), jnp.bfloat16),
            pltpu.VMEM((deep, nc * own), jnp.bfloat16),
            pltpu.VMEM((cols, deep), jnp.bfloat16),
            pltpu.VMEM((nc * own, deep), jnp.bfloat16),
            pltpu.VMEM((row_blocks, LANES), jnp.float32),
            pltpu.VMEM((row_blocks, LANES), jnp.float32),
            pltpu.VMEM((ITERS, nc, row_blocks, LANES), jnp.float32),
            pltpu.VMEM((ITERS, nr, col_blocks, LANES), jnp.float32),
            pltpu.SemaphoreType.DMA((nc - 1,)),
            pltpu.SemaphoreType.DMA((nc - 1,)),
            pltpu.SemaphoreType.DMA((ITERS, nc - 1)),
            pltpu.SemaphoreType.DMA((ITERS, nc - 1)),
            pltpu.SemaphoreType.DMA((ITERS, nr - 1)),
            pltpu.SemaphoreType.DMA((ITERS, nr - 1)),
        ],
        compiler_params=pltpu.CompilerParams(
            collective_id=0, has_side_effects=True, vmem_limit_bytes=48 * 1024 * 1024
        ),
    )(
        hbm(sources),
        hbm(log_source_mass.reshape(own // LANES, LANES)),
        hbm(targets),
        hbm(log_target_mass.reshape(col_blocks, LANES)),
        hbm(start_potential.reshape(col_blocks, LANES)),
    )
    return row.reshape(own), col.reshape(cols)


def hbm(x):
    return pltpu.with_memory_space_constraint(x, pltpu.HBM)


def solution(mesh):
    return jax.shard_map(
        functools.partial(on_device, mesh.shape["row"], mesh.shape["col"]),
        mesh=mesh,
        in_specs=(P(None, ("row", "col")), P(("row", "col")), P(None, "col"), P("col"), P("col")),
        out_specs=(P(("row", "col")), P("col")),
        check_vma=False,
    )
```
